128 devices in a mesh: dp: 8 (over y, core), ctx: 16 (over x, z).
Axes of the slice: x: 4, y: 4, z: 4, core: 2. Of those that a mesh axis runs over, the one named last changes fastest.
Arguments:
- queries: bfloat16 [8, 4096, 2048], P('dp', 'ctx'), may hold values from -6 to 6
- keys: bfloat16 [8, 4096, 2048], P('dp', 'ctx'), may hold values from -6 to 6
- values: bfloat16 [8, 4096, 2048], P('dp', 'ctx'), may hold values from -6 to 6
- out_weight: bfloat16 [2048, 2048], replicated, may hold values from -0.125 to 0.125
- grad_out: bfloat16 [8, 4096, 2048], P('dp', 'ctx'), may hold values from -6 to 6
- tile_docs: int32 [8, 32], P('dp', 'ctx'), may hold values from 0 to 9, never falling along the last dimension, each value on 1 to 8 neighbouring positions
Outputs:
- layer_out: bfloat16 [8, 4096, 2048], P('dp', 'ctx')
- grad_queries: bfloat16 [8, 4096, 2048], P('dp', 'ctx')
- grad_keys: bfloat16 [8, 4096, 2048], P('dp', 'ctx')
- grad_values: bfloat16 [8, 4096, 2048], P('dp', 'ctx')
- grad_weight: float32 [2048, 2048], P('dp', 'ctx')
The draws below stay inside these ranges and needn't reach their ends.
Inputs may be any that keep to these rules, and one draw needn't show every extreme that they name: `tile_docs`: along each sequence the document number never falls from tile to tile; every document covers 1 to 8 tiles, and one document of every sequence covers exactly 8.
All inputs are finite; a program needn't handle non-finite values.
Results may differ from the reference program's by a relative error of at most 0.0058.
Values sent between devices are 32-bit elements; how exact they have to be, the bound alone decides.
No kernel may reach another device: no remote copies, remote signals or barrier semaphores. Data moves between devices by JAX's collectives and lax.ppermute only.
A program may use at most 128 MiB of HBM per device.

```python
import math
import jax
import jax.numpy as jnp
import numpy as np
from jax import lax

D = 2048
HEADS = 16
HDIM = 128
TILE = 128
HD = 2048
BATCH = 8
LENGTH = 4096
NTILES = 32
DOCS = 10
MOST_TILES = 8


def block_levels(own_key, dims, split, low, top_value):
    def one(position, blocks):
        draws = jax.random.uniform(jax.random.fold_in(jax.random.fold_in(own_key, 6), position), (blocks,), jnp.float32, low / len(split), top_value / len(split))
        return jnp.repeat(jnp.exp(draws), dims[position] // blocks).reshape((-1,) + (1,) * (len(dims) - position - 1))

    gain = one(*split[0])
    for cut in split[1:]:
        gain = gain * one(*cut)
    return gain


def profile(count, total, limit, slope):
    loads = [(1 << 20) // math.isqrt(grade ** slope) + 1 for grade in range(2, count + 1)]
    surplus, holding = total - limit - (count - 1), [1] * (count - 1)
    while surplus > 0:
        free = [i for i in range(count - 1) if holding[i] < limit]
        mass, left = sum([loads[i] for i in free]), surplus
        for i in free:
            more = min(limit - holding[i], max(1, left * loads[i] // mass), surplus)
            holding[i] = holding[i] + more
            surplus = surplus - more
    return np.array([limit] + holding)


def uneven(own_key, number_of, total, bound, skew):
    if number_of == 2:
        one = jax.random.randint(own_key, (), max(1, total - bound), min(bound, total - 1) + 1)
        return jnp.stack([one, total - one])
    lengths = jnp.asarray(profile(number_of, total, bound, skew), jnp.int32)
    pairs = (number_of - 1) // 2
    source_of, taker = lengths[1:1 + 2 * pairs:2], lengths[2:2 + 2 * pairs:2]
    margin = jnp.minimum(source_of - 1, bound - taker)
    shifted = jax.random.randint(jax.random.fold_in(own_key, 1), (pairs,), 0, 1 << 20) % (margin + 1)
    lengths = lengths.at[1:1 + 2 * pairs:2].set(source_of - shifted).at[2:2 + 2 * pairs:2].set(taker + shifted)
    return lengths[jax.random.permutation(jax.random.fold_in(own_key, 2), number_of)]


def scatter_about(key, extent, scale, bound, pieces=(), held_as=jnp.bfloat16):
    factor_of = block_levels(key, extent, pieces, -0.22, 0.18) if pieces else 1.0
    drawn = jax.random.normal(key, extent, jnp.float32) * scale * factor_of
    return jnp.minimum(jnp.maximum(drawn, -bound), bound).astype(held_as)


def setup_inputs(seed: int = 0) -> dict:
    arg_keys = jax.random.split(jax.random.key(seed), 7)
    return {
        "queries": scatter_about(arg_keys[0], (BATCH, LENGTH, HD), 1.0, 6.0, ((0, 8), (1, 16))),
        "keys": scatter_about(arg_keys[1], (BATCH, LENGTH, HD), 1.0, 6.0, ((0, 8), (1, 16))),
        "values": scatter_about(arg_keys[2], (BATCH, LENGTH, HD), 1.0, 6.0, ((0, 8), (1, 16))),
        "out_weight": scatter_about(arg_keys[3], (HD, D), HD ** -0.5, 0.125),
        "grad_out": scatter_about(arg_keys[4], (BATCH, LENGTH, D), 1.0, 6.0, ((0, 8), (1, 16))),
        "tile_docs": jax.vmap(lambda own: jnp.searchsorted(jnp.cumsum(uneven(own, DOCS, NTILES, MOST_TILES, 2)), jnp.arange(NTILES), side="right"))(jax.random.split(arg_keys[5], BATCH)).reshape((BATCH, NTILES)).astype(jnp.int32),
    }


def one_sequence(queries, keys, values, grad_out, tile_docs, out_weight):
    tiles = LENGTH // TILE
    scale = 1.0 / HDIM
    q = queries.reshape(tiles, TILE, HEADS, HDIM).astype(jnp.float32)
    k = keys.reshape(tiles, TILE, HEADS, HDIM).astype(jnp.float32)
    v = values.reshape(tiles, TILE, HEADS, HDIM).astype(jnp.float32)
    rows = lax.broadcasted_iota(jnp.int32, (TILE, TILE), 0)
    cols = lax.broadcasted_iota(jnp.int32, (TILE, TILE), 1)
    causal = rows >= cols
    scores = jnp.einsum("ntha,nsha->nhts", q, k)
    attn_q = (scale * jnp.where(causal, scores, 0.0)).astype(jnp.bfloat16)
    kv = jnp.einsum("ntha,nthc->nhac", k, v)
    empty = jnp.zeros((HEADS, HDIM, HDIM), jnp.float32)

    def carry_step(carry, item):
        state, prev = carry
        block, ident = item
        excl = jnp.where(ident == prev, state, jnp.zeros_like(state))
        return (excl + block, ident), excl

    _, state = lax.scan(carry_step, (empty, jnp.int32(-1)), (kv, tile_docs))
    state_b = (scale * state).astype(jnp.bfloat16)
    out_tiles = jnp.einsum("nhts,nshc->nthc", attn_q.astype(jnp.float32), v)
    out_tiles = out_tiles + jnp.einsum("ntha,nhac->nthc", q, state_b.astype(jnp.float32))
    attended = out_tiles.astype(jnp.bfloat16).reshape(LENGTH, HD)
    layer_out = jnp.dot(attended, out_weight, preferred_element_type=jnp.float32).astype(jnp.bfloat16)
    grad_att = jnp.dot(grad_out, out_weight.T, preferred_element_type=jnp.float32).astype(jnp.bfloat16)
    g = grad_att.reshape(tiles, TILE, HEADS, HDIM).astype(jnp.float32)
    qg = jnp.einsum("ntha,nthc->nhca", q, g)
    _, rev = lax.scan(carry_step, (empty, jnp.int32(-1)), (qg, tile_docs), reverse=True)
    rev_b = (scale * rev).astype(jnp.bfloat16).astype(jnp.float32)
    attn_g = (scale * jnp.where(causal, jnp.einsum("nthc,nshc->nhts", g, v), 0.0)).astype(jnp.bfloat16)
    attn_g = attn_g.astype(jnp.float32)
    attn_qf = attn_q.astype(jnp.float32)
    state_f = state_b.astype(jnp.float32)
    grad_q = jnp.einsum("nhts,nsha->ntha", attn_g, k) + jnp.einsum("nthc,nhac->ntha", g, state_f)
    grad_k = jnp.einsum("nhts,ntha->nsha", attn_g, q) + jnp.einsum("nshc,nhca->nsha", v, rev_b)
    grad_v = jnp.einsum("nhts,nthc->nshc", attn_qf, g) + jnp.einsum("nsha,nhca->nshc", k, rev_b)
    shaped = lambda x: x.astype(jnp.bfloat16).reshape(LENGTH, HD)
    return layer_out, shaped(grad_q), shaped(grad_k), shaped(grad_v), attended


def reference(queries, keys, values, out_weight, grad_out, tile_docs):
    def per_row(items):
        return one_sequence(items[0], items[1], items[2], items[3], items[4], out_weight)

    layer_out, grad_q, grad_k, grad_v, attended = lax.map(per_row, (queries, keys, values, grad_out, tile_docs))
    flat_att = attended.reshape(BATCH * LENGTH, HD)
    flat_grad = grad_out.reshape(BATCH * LENGTH, D)
    grad_weight = jnp.dot(flat_att.T, flat_grad, preferred_element_type=jnp.float32)
    grad_weight = grad_weight * (1.0 / (BATCH * LENGTH) ** 0.5)
    return layer_out, grad_q, grad_k, grad_v, grad_weight
```

```python
import functools

import jax
import jax.numpy as jnp
from jax import lax
from jax.experimental import pallas as pl
from jax.experimental.pallas import tpu as pltpu
from jax.sharding import Mesh
from jax.sharding import PartitionSpec as P

HEADS = 16
HDIM = 128
TILE = 128
TOKENS = 2 * TILE
BLOCKS = 16
ROWS = HDIM + 8
SCALE = 1.0 / HDIM
F32 = jnp.float32
BF16 = jnp.bfloat16
VMEM = 60 * 1024 * 1024
WEIGH = 100


def mul(a, b, da, db):
    return lax.dot_general(a, b, (((da,), (db,)), ((), ())), preferred_element_type=F32)


def params():
    return pltpu.CompilerParams(vmem_limit_bytes=VMEM)


def cost(flops, moved):
    return pl.CostEstimate(flops=int(flops) // WEIGH, bytes_accessed=int(moved) // WEIGH, transcendentals=0)


def whole(shape):
    return pl.BlockSpec(shape, lambda *_: (0,) * len(shape))


SMEM = pl.BlockSpec(memory_space=pltpu.SMEM)


def put_ends(ref, head, docs):
    ref[head, HDIM : HDIM + 1, :] = jnp.full((1, HDIM), docs[0, 0], jnp.int32).astype(F32)
    ref[head, HDIM + 1 : HDIM + 2, :] = jnp.full((1, HDIM), docs[0, 1], jnp.int32).astype(F32)
    ref[head, HDIM + 2 :, :] = jnp.zeros((ROWS - HDIM - 2, HDIM), F32)


def joined(x, keep, first):
    rows = lax.broadcasted_iota(jnp.int32, x.shape, 0)
    return jnp.where(keep | ((rows >= TILE) if first else (rows < TILE)), x, jnp.zeros_like(x))


def trailing_kernel(docs, k, v, out):
    kv = mul(joined(k[...], docs[0, 0] == docs[0, 1], True), v[...], 0, 0)
    for head in range(2):
        part = slice(head * HDIM, (head + 1) * HDIM)
        out[head, :HDIM, :] = kv[part, part]
        put_ends(out, head, docs)


def leading_kernel(docs, grad_out, weight, q, g, out):
    grad = mul(grad_out[...], weight[...], 1, 1).astype(BF16)
    g[...] = grad
    qg = mul(joined(grad, docs[0, 0] == docs[0, 1], False), q[...], 0, 0)
    for head in range(2):
        part = slice(head * HDIM, (head + 1) * HDIM)
        out[head, :HDIM, :] = qg[part, part]
        put_ends(out, head, docs)


def scan_kernel(reverse, part, out):
    carried = jnp.zeros((HDIM, HDIM), F32)
    near = jnp.full((1, HDIM), -1.0, F32)
    order = range(BLOCKS - 1, -1, -1) if reverse else range(BLOCKS)
    for block in order:
        first = part[block, HDIM : HDIM + 1, :]
        last = part[block, HDIM + 1 : HDIM + 2, :]
        entry, leave = (last, first) if reverse else (first, last)
        state = jnp.where(near == entry, carried, 0.0)
        out[block] = state
        carried = part[block, :HDIM, :] + jnp.where(first == last, state, 0.0)
        near = leave


def causal(same):
    rows = lax.broadcasted_iota(jnp.int32, (TOKENS, TOKENS), 0)
    cols = lax.broadcasted_iota(jnp.int32, (TOKENS, TOKENS), 1)
    return (rows >= cols) & (same | (rows < TILE) | (cols >= TILE))


def attended_kernel(place, docs, q, k, v, state, low, high, out, far, up, own, down, turned):
    del place
    step = pl.program_id(0)
    width = low.shape[1]
    up[:, pl.ds(pl.multiple_of(step * width, width), width)] = low[...]
    down[:, pl.ds(pl.multiple_of(step * width, width), width)] = high[...]
    same = docs[0, 0] == docs[0, 1]
    mask = causal(same)
    for head in range(state.shape[0]):
        cols = slice(head * HDIM, (head + 1) * HDIM)
        query = q[:, cols]
        attn = jnp.where(mask, SCALE * mul(query, k[:, cols], 1, 1), 0.0).astype(BF16)
        got = mul(attn, v[:, cols], 1, 0)
        got = got + mul(joined(query, same, False), (SCALE * state[head]).astype(BF16), 1, 0)
        got = got.astype(BF16)
        out[:, cols] = got
        turned[cols, :] = got.astype(F32).T

    @pl.when(step == 0)
    def _():
        far[...] = turned[...]

    @pl.when(step == 2)
    def _():
        own[...] = turned[...].astype(BF16)

    for when, wide in ((1, up), (3, down)):

        @pl.when(step == when)
        def _(wide=wide):
            for head in range(4):
                start = 4 * width + head * TOKENS
                wide[:, start : start + TOKENS] = turned[head * HDIM : (head + 1) * HDIM, :]


def grads_kernel(docs, q, k, v, g, state, rev, gq, gk, gv):
    same = docs[0, 0] == docs[0, 1]
    mask = causal(same)
    for head in range(state.shape[0]):
        cols = slice(head * HDIM, (head + 1) * HDIM)
        qh, kh, vh, gh = q[:, cols], k[:, cols], v[:, cols], g[:, cols]
        attn_q = jnp.where(mask, SCALE * mul(qh, kh, 1, 1), 0.0).astype(BF16)
        attn_g = jnp.where(mask, SCALE * mul(gh, vh, 1, 1), 0.0).astype(BF16)
        state_b = (SCALE * state[head]).astype(BF16)
        rev_b = (SCALE * rev[head]).astype(BF16)
        gq[:, cols] = (mul(attn_g, kh, 1, 0) + mul(joined(gh, same, False), state_b, 1, 1)).astype(BF16)
        gk[:, cols] = (mul(attn_g, qh, 0, 0) + mul(joined(vh, same, True), rev_b, 1, 0)).astype(BF16)
        gv[:, cols] = (mul(attn_q, gh, 0, 0) + mul(joined(kh, same, True), rev_b, 1, 1)).astype(BF16)


def product_kernel(side, att_own, att_far, att_low, att_high, own, low_a, low_b, high_a, high_b, far_a, far_b, out, left, right):
    del side

    @pl.when(pl.program_id(0) == 0)
    def _():
        left[:, :TOKENS] = att_own[...]
        for i, att in enumerate((att_low, att_high)):
            cols = slice((i + 1) * TOKENS, (i + 2) * TOKENS)
            left[:HDIM, cols] = att[:, :TOKENS].astype(BF16)
            left[HDIM:, cols] = att[:, TOKENS:].astype(BF16)
        left[:, 3 * TOKENS :] = att_far[...].astype(BF16)

    right[:TOKENS] = own[...]
    for i, other in enumerate((low_a, low_b, high_a, high_b, far_a, far_b)):
        right[TOKENS + i * TILE : TOKENS + (i + 1) * TILE] = other[...].astype(BF16)
    total = mul(left[...], right[...], 1, 0)
    for block in range(out.shape[0]):
        out[block] = total[:, block * HDIM : (block + 1) * HDIM]


def product(att_own, att_far, own, low, high, up, down, side):
    width = own.shape[1]
    step = 4 * HDIM
    rows = pl.BlockSpec((TOKENS, TOKENS), lambda i, w: (w[0], 0))
    packed = pl.BlockSpec((TILE, 2 * TOKENS), lambda i, w: (0, width // (2 * TOKENS) + w[0]))

    def cols(count):
        return pl.BlockSpec((count, step), lambda i, w: (0, i))

    spec = pltpu.PrefetchScalarGridSpec(
        num_scalar_prefetch=1,
        grid=(width // step,),
        in_specs=[rows, rows, packed, packed, cols(TOKENS)] + [cols(TILE)] * 6,
        out_specs=pl.BlockSpec((step // HDIM, TOKENS, HDIM), lambda i, w: (i, 0, 0)),
        scratch_shapes=[pltpu.VMEM((TOKENS, 4 * TOKENS), BF16), pltpu.VMEM((4 * TOKENS, step), BF16)],
    )
    return pl.pallas_call(
        product_kernel,
        grid_spec=spec,
        out_shape=jax.ShapeDtypeStruct((width // HDIM, TOKENS, HDIM), F32),
        compiler_params=params(),
        cost_estimate=cost(2 * 256 * 1024 * width, 4 * width * 1024),
        name="product",
    )(side.astype(jnp.int32).reshape(1), att_own, att_far, up, down, own, *low, *high, up, down)


def ring(step):
    return [(i, (i + step) % 4) for i in range(4)]


def body(queries, keys, values, weight, grad_out, docs):
    ctx = ("x", "z")
    q, k, v, go = queries[0], keys[0], values[0], grad_out[0]
    width = q.shape[1]
    factor = 1.0 / float(TOKENS * 128) ** 0.5

    top, bottom = go[:TILE].astype(F32), go[TILE:].astype(F32)
    top, bottom, k, v = lax.optimization_barrier((top, bottom, k, v))
    low_top = lax.ppermute(top, "y", ring(1))
    high_bottom = lax.ppermute(bottom, "y", ring(-1))
    low_bottom = lax.ppermute(bottom, "y", ring(1))
    high_top = lax.ppermute(top, "y", ring(-1))

    per = 2
    block = pl.BlockSpec((TOKENS, per * HDIM), lambda i: (0, i))
    summed = pl.BlockSpec((per, ROWS, HDIM), lambda i: (i, 0, 0))
    matrix = pl.BlockSpec((per, HDIM, HDIM), lambda i: (i, 0, 0))
    tokens = jax.ShapeDtypeStruct((TOKENS, width), BF16)
    payload = jax.ShapeDtypeStruct((HEADS, ROWS, HDIM), F32)

    trailing = pl.pallas_call(
        trailing_kernel,
        grid=(HEADS // per,),
        in_specs=[SMEM, block, block],
        out_specs=summed,
        out_shape=payload,
        compiler_params=params(),
        cost_estimate=cost(2 * 32 * 128**3, 3 << 20),
        name="trailing",
    )(docs, k, v)
    by_head = lax.all_to_all(trailing, ctx, 0, 0, tiled=True)

    g, leading = pl.pallas_call(
        leading_kernel,
        grid=(HEADS // per,),
        in_specs=[
            SMEM,
            whole((TOKENS, width)),
            pl.BlockSpec((per * HDIM, width), lambda i: (i, 0)),
            block,
        ],
        out_specs=[block, summed],
        out_shape=[tokens, payload],
        compiler_params=params(),
        cost_estimate=cost(2 * 256 * 2048 * 2048, 12 << 20),
        name="leading",
    )(docs, go, weight, q)

    def scan(parts, reverse):
        return pl.pallas_call(
            functools.partial(scan_kernel, reverse),
            out_shape=jax.ShapeDtypeStruct((BLOCKS, HDIM, HDIM), F32),
            compiler_params=params(),
            cost_estimate=cost(1 << 20, 2 << 20),
            name="scan",
        )(parts)

    by_head, leading, low_top, high_bottom = lax.optimization_barrier((by_head, leading, low_top, high_bottom))
    state = lax.all_to_all(scan(by_head, False), ctx, 0, 0, tiled=True)
    state, low_bottom, high_top = lax.optimization_barrier((state, low_bottom, high_top))

    def group(i, w):
        return (w[0] + 6 - i) % 4

    place = lax.axis_index("y").astype(jnp.int32).reshape(1)
    four = pl.BlockSpec((TOKENS, 4 * HDIM), lambda i, w: (0, group(i, w)))
    passed = pl.BlockSpec((TILE, 4 * HDIM), lambda i, w: (0, i))
    turned = jax.ShapeDtypeStruct((4 * HDIM, TOKENS), F32)
    packed = jax.ShapeDtypeStruct((TILE, width + 4 * TOKENS), F32)
    attended, far, up, att_own, down = pl.pallas_call(
        attended_kernel,
        grid_spec=pltpu.PrefetchScalarGridSpec(
            num_scalar_prefetch=1,
            grid=(HEADS // 4,),
            in_specs=[SMEM, four, four, four, pl.BlockSpec((4, HDIM, HDIM), lambda i, w: (group(i, w), 0, 0))]
            + [passed, passed],
            out_specs=[four] + [pl.BlockSpec(part.shape, lambda i, w: (0, 0)) for part in (turned, packed, turned, packed)],
            scratch_shapes=[pltpu.VMEM((4 * HDIM, TOKENS), F32)],
        ),
        out_shape=[tokens, turned, packed, jax.ShapeDtypeStruct(turned.shape, BF16), packed],
        compiler_params=params(),
        cost_estimate=cost(2 * 32 * 4 * 128**3, 7 << 20),
        name="attended",
    )(place, docs, q, k, v, state, low_top, high_bottom)
    leading, attended = lax.optimization_barrier((leading, attended))
    rev_by_head = lax.all_to_all(leading, ctx, 0, 0, tiled=True)
    up = lax.ppermute(up, "y", ring(1))
    down = lax.ppermute(down, "y", ring(-1))
    far = lax.ppermute(far, "y", ring(2))
    rev_by_head, far = lax.optimization_barrier((rev_by_head, far))
    rev_scan = scan(rev_by_head, True)

    layer_out = jnp.dot(attended, weight, preferred_element_type=F32).astype(BF16)

    core = lax.axis_index("core")
    rev = lax.all_to_all(rev_scan, ctx, 0, 0, tiled=True)
    far, rev = lax.optimization_barrier((far, rev))
    pieces = (att_own, far, go, (low_top, low_bottom), (high_top, high_bottom), up, down)
    given = product(*pieces, 1 - core)
    kept = product(*pieces, core)
    taken = lax.ppermute(given, "core", [(0, 1), (1, 0)])
    spread = lax.all_to_all((kept + taken) * factor, ctx, 0, 0, tiled=True)
    grad_weight = jnp.sum(spread, axis=0)

    grad_q, grad_k, grad_v = pl.pallas_call(
        grads_kernel,
        grid=(HEADS // per,),
        in_specs=[SMEM, block, block, block, block, matrix, matrix],
        out_specs=[block, block, block],
        out_shape=[tokens, tokens, tokens],
        compiler_params=params(),
        cost_estimate=cost(2 * 32 * 10 * 128**3, 9 << 20),
        name="grads",
    )(docs, q, k, v, g, state, rev)
    return layer_out[None], grad_q[None], grad_k[None], grad_v[None], grad_weight


def solution(mesh):
    fine = Mesh(mesh.devices.reshape(4, 2, 4, 4), ("y", "core", "x", "z"))
    dp, ctx = ("y", "core"), ("x", "z")
    tokens = P(dp, ctx, None)
    return jax.shard_map(
        body,
        mesh=fine,
        in_specs=(tokens, tokens, tokens, P(), tokens, P(dp, ctx)),
        out_specs=(tokens, tokens, tokens, tokens, P(dp, ctx)),
        check_vma=False,
    )
```

```python
import functools

import jax
import jax.numpy as jnp
from jax import lax
from jax.experimental import pallas as pl
from jax.experimental.pallas import tpu as pltpu
from jax.sharding import Mesh
from jax.sharding import PartitionSpec as P

HEADS = 16
HDIM = 128
TILE = 128
TOKENS = 2 * TILE
BLOCKS = 16
ROWS = HDIM + 8
SCALE = 1.0 / HDIM
F32 = jnp.float32
BF16 = jnp.bfloat16
VMEM = 60 * 1024 * 1024
SMALL = 24 * 1024 * 1024
WEIGH = 100


def mul(a, b, da, db):
    return lax.dot_general(a, b, (((da,), (db,)), ((), ())), preferred_element_type=F32)


def params(limit=VMEM):
    return pltpu.CompilerParams(vmem_limit_bytes=limit)


def cost(flops, moved):
    return pl.CostEstimate(flops=int(flops) // WEIGH, bytes_accessed=int(moved) // WEIGH, transcendentals=0)


def whole(shape):
    return pl.BlockSpec(shape, lambda *_: (0,) * len(shape))


SMEM = pl.BlockSpec(memory_space=pltpu.SMEM)


def put_ends(ref, head, docs):
    ref[head, HDIM : HDIM + 1, :] = jnp.full((1, HDIM), docs[0, 0], jnp.int32).astype(F32)
    ref[head, HDIM + 1 : HDIM + 2, :] = jnp.full((1, HDIM), docs[0, 1], jnp.int32).astype(F32)
    ref[head, HDIM + 2 :, :] = jnp.zeros((ROWS - HDIM - 2, HDIM), F32)


def joined(x, keep, first):
    rows = lax.broadcasted_iota(jnp.int32, x.shape, 0)
    return jnp.where(keep | ((rows >= TILE) if first else (rows < TILE)), x, jnp.zeros_like(x))


def trailing_kernel(docs, k, v, out):
    same = docs[0, 0] == docs[0, 1]
    for pair in range(out.shape[0] // 2):
        cols = slice(2 * pair * HDIM, 2 * (pair + 1) * HDIM)
        kv = mul(joined(k[:, cols], same, True), v[:, cols], 0, 0)
        for head in range(2):
            part = slice(head * HDIM, (head + 1) * HDIM)
            out[2 * pair + head, :HDIM, :] = kv[part, part]
            put_ends(out, 2 * pair + head, docs)


def leading_kernel(docs, grad_out, weight, q, g, out):
    grad = mul(grad_out[...], weight[...], 1, 1).astype(BF16)
    g[...] = grad
    qg = mul(joined(grad, docs[0, 0] == docs[0, 1], False), q[...], 0, 0)
    for head in range(2):
        part = slice(head * HDIM, (head + 1) * HDIM)
        out[head, :HDIM, :] = qg[part, part]
        put_ends(out, head, docs)


def scan_kernel(reverse, part, *rest):
    out = rest[-1]
    base = part.shape[1] - ROWS
    carried = jnp.zeros((HDIM, HDIM), F32)
    near = jnp.full((1, HDIM), -1.0, F32)
    order = range(BLOCKS - 1, -1, -1) if reverse else range(BLOCKS)
    for block in order:
        first = part[block, base + HDIM : base + HDIM + 1, :]
        last = part[block, base + HDIM + 1 : base + HDIM + 2, :]
        entry, leave = (last, first) if reverse else (first, last)
        state = jnp.where(near == entry, carried, 0.0)
        out[block, :HDIM, :] = state
        carried = part[block, base : base + HDIM, :] + jnp.where(first == last, state, 0.0)
        near = leave
    for along in rest[:-1]:
        out[:, HDIM:, :] = along[...]


def causal(same):
    rows = lax.broadcasted_iota(jnp.int32, (TOKENS, TOKENS), 0)
    cols = lax.broadcasted_iota(jnp.int32, (TOKENS, TOKENS), 1)
    return (rows >= cols) & (same | (rows < TILE) | (cols >= TILE))


def attended_kernel(place, docs, q, k, v, state, out, far, up, own, down, turned):
    del place
    step = pl.program_id(0)
    same = docs[0, 0] == docs[0, 1]
    mask = causal(same)
    for head in range(state.shape[0]):
        cols = slice(head * HDIM, (head + 1) * HDIM)
        query = q[:, cols]
        attn = jnp.where(mask, SCALE * mul(query, k[:, cols], 1, 1), 0.0).astype(BF16)
        got = mul(attn, v[:, cols], 1, 0)
        got = got + mul(joined(query, same, False), (SCALE * state[head]).astype(BF16), 1, 0)
        got = got.astype(BF16)
        out[:, cols] = got
        turned[cols, :] = got.astype(F32).T

    for when, wide in enumerate((far, up, own, down)):

        @pl.when(step == when)
        def _(wide=wide):
            wide[...] = turned[...].astype(wide.dtype)


def grads_kernel(docs, q, k, v, g, state, rev, gq, gk, gv):
    same = docs[0, 0] == docs[0, 1]
    mask = causal(same)
    for head in range(state.shape[0]):
        cols = slice(head * HDIM, (head + 1) * HDIM)
        qh, kh, vh, gh = q[:, cols], k[:, cols], v[:, cols], g[:, cols]
        attn_q = jnp.where(mask, SCALE * mul(qh, kh, 1, 1), 0.0).astype(BF16)
        attn_g = jnp.where(mask, SCALE * mul(gh, vh, 1, 1), 0.0).astype(BF16)
        state_b = (SCALE * state[head]).astype(BF16)
        rev_b = (SCALE * rev[head]).astype(BF16)
        gq[:, cols] = (mul(attn_g, kh, 1, 0) + mul(joined(gh, same, False), state_b, 1, 1)).astype(BF16)
        gk[:, cols] = (mul(attn_g, qh, 0, 0) + mul(joined(vh, same, True), rev_b, 1, 0)).astype(BF16)
        gv[:, cols] = (mul(attn_q, gh, 0, 0) + mul(joined(kh, same, True), rev_b, 1, 1)).astype(BF16)


def pack_kernel(own, *rest):
    others, out = rest[:-1], rest[-1]
    out[:TOKENS] = own[...]
    start = TOKENS
    for other in others:
        out[start : start + other.shape[0]] = other[...].astype(BF16)
        start += other.shape[0]


def pack(own, others):
    width = own.shape[1]
    step = 4 * HDIM

    def cols(count):
        return pl.BlockSpec((count, step), lambda i: (0, i))

    return pl.pallas_call(
        pack_kernel,
        grid=(width // step,),
        in_specs=[cols(TOKENS)] + [cols(other.shape[0]) for other in others],
        out_specs=cols(4 * TOKENS),
        out_shape=jax.ShapeDtypeStruct((4 * TOKENS, width), BF16),
        compiler_params=params(SMALL),
        cost_estimate=cost(1 << 20, 12 << 20),
        name="pack",
    )(own, *others)


def product_kernel(side, att_own, att_low, att_high, att_far, gathered, out, left):
    del side

    @pl.when(pl.program_id(0) == 0)
    def _():
        for i, att in enumerate((att_own, att_low, att_high, att_far)):
            left[:, i * TOKENS : (i + 1) * TOKENS] = att[...].astype(BF16)

    total = mul(left[...], gathered[...], 1, 0)
    for block in range(out.shape[0]):
        out[block] = total[:, block * HDIM : (block + 1) * HDIM]


def product(atts, gathered, side):
    width = gathered.shape[1]
    step = 4 * HDIM
    rows = pl.BlockSpec((TOKENS, TOKENS), lambda i, w: (w[0], 0))
    spec = pltpu.PrefetchScalarGridSpec(
        num_scalar_prefetch=1,
        grid=(width // step,),
        in_specs=[rows] * 4 + [pl.BlockSpec((4 * TOKENS, step), lambda i, w: (0, i))],
        out_specs=pl.BlockSpec((step // HDIM, TOKENS, HDIM), lambda i, w: (i, 0, 0)),
        scratch_shapes=[pltpu.VMEM((TOKENS, 4 * TOKENS), BF16)],
    )
    return pl.pallas_call(
        product_kernel,
        grid_spec=spec,
        out_shape=jax.ShapeDtypeStruct((width // HDIM, TOKENS, HDIM), F32),
        compiler_params=params(SMALL),
        cost_estimate=cost(2 * 256 * 1024 * width, 4 * width * 1024),
        name="product",
    )(side.astype(jnp.int32).reshape(1), *atts, gathered)


def ring(step):
    return [(i, (i + step) % 4) for i in range(4)]


def body(queries, keys, values, weight, grad_out, docs):
    ctx = ("x", "z")
    q, k, v, go = queries[0], keys[0], values[0], grad_out[0]
    width = q.shape[1]
    factor = 1.0 / float(TOKENS * 128) ** 0.5

    half = TILE // 2
    cuts = [go[half * i : half * (i + 1)].astype(F32) for i in range(4)]
    top, bottom = go[:TILE].astype(F32), go[TILE:].astype(F32)
    top, bottom, cuts, k, v = lax.optimization_barrier((top, bottom, cuts, k, v))
    low_top = lax.ppermute(top, "y", ring(1))
    high_bottom = lax.ppermute(bottom, "y", ring(-1))
    low_middle = lax.ppermute(cuts[2], "y", ring(1))
    high_middle = lax.ppermute(cuts[1], "y", ring(-1))
    low_rest = lax.ppermute(cuts[3], "y", ring(1))
    high_rest = lax.ppermute(cuts[0], "y", ring(-1))

    per = 2
    block = pl.BlockSpec((TOKENS, per * HDIM), lambda i: (0, i))
    summed = pl.BlockSpec((per, ROWS, HDIM), lambda i: (i, 0, 0))
    matrix = pl.BlockSpec((per, HDIM, HDIM), lambda i: (i, 0, 0))
    tokens = jax.ShapeDtypeStruct((TOKENS, width), BF16)
    payload = jax.ShapeDtypeStruct((HEADS, ROWS, HDIM), F32)

    trailing = pl.pallas_call(
        trailing_kernel,
        grid=(HEADS // 4,),
        in_specs=[SMEM] + [pl.BlockSpec((TOKENS, 4 * HDIM), lambda i: (0, i))] * 2,
        out_specs=pl.BlockSpec((4, ROWS, HDIM), lambda i: (i, 0, 0)),
        out_shape=payload,
        compiler_params=params(),
        cost_estimate=cost(2 * 32 * 128**3, 3 << 20),
        name="trailing",
    )(docs, k, v)
    by_head = lax.all_to_all(trailing, ctx, 0, 0, tiled=True)

    g, leading = pl.pallas_call(
        leading_kernel,
        grid=(HEADS // per,),
        in_specs=[
            SMEM,
            whole((TOKENS, width)),
            pl.BlockSpec((per * HDIM, width), lambda i: (i, 0)),
            block,
        ],
        out_specs=[block, summed],
        out_shape=[tokens, payload],
        compiler_params=params(),
        cost_estimate=cost(2 * 256 * 2048 * 2048, 12 << 20),
        name="leading",
    )(docs, go, weight, q)

    def scan(reverse, *parts):
        return pl.pallas_call(
            functools.partial(scan_kernel, reverse),
            out_shape=jax.ShapeDtypeStruct((BLOCKS, HDIM + ROWS * (len(parts) - 1), HDIM), F32),
            compiler_params=params(SMALL),
            cost_estimate=cost(1 << 20, 2 << 20),
            name="scan",
        )(*parts)

    by_head, leading, low_top, high_bottom, low_middle, high_middle = lax.optimization_barrier(
        (by_head, leading, low_top, high_bottom, low_middle, high_middle)
    )
    far_top = lax.ppermute(low_top, "y", ring(1))
    far_bottom = lax.ppermute(high_bottom, "y", ring(-1))
    both = lax.all_to_all(scan(False, by_head, leading), ctx, 0, 0, tiled=True)
    both, low_rest, high_rest = lax.optimization_barrier((both, low_rest, high_rest))

    def group(i, w):
        return (w[0] + 6 - i) % 4

    place = lax.axis_index("y").astype(jnp.int32).reshape(1)
    four = pl.BlockSpec((TOKENS, 4 * HDIM), lambda i, w: (0, group(i, w)))
    turned = jax.ShapeDtypeStruct((4 * HDIM, TOKENS), F32)
    attended, far, up, att_own, down = pl.pallas_call(
        attended_kernel,
        grid_spec=pltpu.PrefetchScalarGridSpec(
            num_scalar_prefetch=1,
            grid=(HEADS // 4,),
            in_specs=[SMEM, four, four, four, pl.BlockSpec((4, HDIM, HDIM), lambda i, w: (group(i, w), 0, 0))],
            out_specs=[four] + [pl.BlockSpec(part.shape, lambda i, w: (0, 0)) for part in (turned,) * 4],
            scratch_shapes=[pltpu.VMEM((4 * HDIM, TOKENS), F32)],
        ),
        out_shape=[tokens, turned, turned, jax.ShapeDtypeStruct(turned.shape, BF16), turned],
        compiler_params=params(),
        cost_estimate=cost(2 * 32 * 4 * 128**3, 7 << 20),
        name="attended",
    )(place, docs, q, k, v, both)
    behind, attended = lax.optimization_barrier((both, attended))
    rev_scan = scan(True, behind)
    rev = lax.all_to_all(rev_scan, ctx, 0, 0, tiled=True)
    far, up, down, far_top, far_bottom = lax.optimization_barrier((far, up, down, far_top, far_bottom))
    far = lax.ppermute(far, "y", ring(2))
    up = lax.ppermute(up, "y", ring(1))
    down = lax.ppermute(down, "y", ring(-1))
    gathered = pack(
        go, (low_top, low_middle, low_rest, high_rest, high_middle, high_bottom, far_top, far_bottom)
    )

    layer_out = jnp.dot(attended, weight, preferred_element_type=F32).astype(BF16)

    core = lax.axis_index("core")
    gathered, rev = lax.optimization_barrier((gathered, rev))
    atts = (att_own, up, down, far)
    given = product(atts, gathered, 1 - core)
    kept = product(atts, gathered, core)
    taken = lax.ppermute(given, "core", [(0, 1), (1, 0)])
    spread = lax.all_to_all((kept + taken) * factor, ctx, 0, 0, tiled=True)
    grad_weight = jnp.sum(spread, axis=0)

    grad_q, grad_k, grad_v = pl.pallas_call(
        grads_kernel,
        grid=(HEADS // per,),
        in_specs=[SMEM, block, block, block, block, matrix, matrix],
        out_specs=[block, block, block],
        out_shape=[tokens, tokens, tokens],
        compiler_params=params(),
        cost_estimate=cost(2 * 32 * 10 * 128**3, 9 << 20),
        name="grads",
    )(docs, q, k, v, g, both, rev)
    return layer_out[None], grad_q[None], grad_k[None], grad_v[None], grad_weight


def solution(mesh):
    fine = Mesh(mesh.devices.reshape(4, 2, 4, 4), ("y", "core", "x", "z"))
    dp, ctx = ("y", "core"), ("x", "z")
    tokens = P(dp, ctx, None)
    return jax.shard_map(
        body,
        mesh=fine,
        in_specs=(tokens, tokens, tokens, P(), tokens, P(dp, ctx)),
        out_specs=(tokens, tokens, tokens, tokens, P(dp, ctx)),
        check_vma=False,
    )
```

```python
import functools

import jax
import jax.numpy as jnp
from jax import lax
from jax.experimental import pallas as pl
from jax.experimental.pallas import tpu as pltpu
from jax.sharding import Mesh
from jax.sharding import PartitionSpec as P

HEADS = 16
HDIM = 128
TILE = 128
TOKENS = 2 * TILE
BLOCKS = 16
ROWS = HDIM + 8
SCALE = 1.0 / HDIM
F32 = jnp.float32
BF16 = jnp.bfloat16
VMEM = 60 * 1024 * 1024
SMALL = 24 * 1024 * 1024
WEIGH = 100
MIDDLE = 48
PRODUCT = 15 << 30


def mul(a, b, da, db):
    return lax.dot_general(a, b, (((da,), (db,)), ((), ())), preferred_element_type=F32)


def params(limit=VMEM):
    return pltpu.CompilerParams(vmem_limit_bytes=limit)


def cost(flops, moved):
    return pl.CostEstimate(flops=int(flops) // WEIGH, bytes_accessed=int(moved) // WEIGH, transcendentals=0)


def whole(shape):
    return pl.BlockSpec(shape, lambda *_: (0,) * len(shape))


SMEM = pl.BlockSpec(memory_space=pltpu.SMEM)


def put_ends(ref, head, docs):
    ref[head, HDIM : HDIM + 1, :] = jnp.full((1, HDIM), docs[0, 0], jnp.int32).astype(F32)
    ref[head, HDIM + 1 : HDIM + 2, :] = jnp.full((1, HDIM), docs[0, 1], jnp.int32).astype(F32)
    ref[head, HDIM + 2 :, :] = jnp.zeros((ROWS - HDIM - 2, HDIM), F32)


def joined(x, keep, first):
    rows = lax.broadcasted_iota(jnp.int32, x.shape, 0)
    return jnp.where(keep | ((rows >= TILE) if first else (rows < TILE)), x, jnp.zeros_like(x))


def trailing_kernel(docs, k, v, out):
    same = docs[0, 0] == docs[0, 1]
    for pair in range(out.shape[0] // 2):
        cols = slice(2 * pair * HDIM, 2 * (pair + 1) * HDIM)
        kv = mul(joined(k[:, cols], same, True), v[:, cols], 0, 0)
        for head in range(2):
            part = slice(head * HDIM, (head + 1) * HDIM)
            out[2 * pair + head, :HDIM, :] = kv[part, part]
            put_ends(out, 2 * pair + head, docs)


def leading_kernel(docs, grad_out, weight, q, g, out):
    grad = mul(grad_out[...], weight[...], 1, 1).astype(BF16)
    g[...] = grad
    qg = mul(joined(grad, docs[0, 0] == docs[0, 1], False), q[...], 0, 0)
    for head in range(2):
        part = slice(head * HDIM, (head + 1) * HDIM)
        out[head, :HDIM, :] = qg[part, part]
        put_ends(out, head, docs)


def scan_kernel(reverse, part, *rest):
    out = rest[-1]
    base = part.shape[1] - ROWS
    carried = jnp.zeros((HDIM, HDIM), F32)
    near = jnp.full((1, HDIM), -1.0, F32)
    order = range(BLOCKS - 1, -1, -1) if reverse else range(BLOCKS)
    for block in order:
        first = part[block, base + HDIM : base + HDIM + 1, :]
        last = part[block, base + HDIM + 1 : base + HDIM + 2, :]
        entry, leave = (last, first) if reverse else (first, last)
        state = jnp.where(near == entry, carried, 0.0)
        out[block, :HDIM, :] = state
        carried = part[block, base : base + HDIM, :] + jnp.where(first == last, state, 0.0)
        near = leave
    for along in rest[:-1]:
        out[:, HDIM:, :] = along[...]


def causal(same):
    rows = lax.broadcasted_iota(jnp.int32, (TOKENS, TOKENS), 0)
    cols = lax.broadcasted_iota(jnp.int32, (TOKENS, TOKENS), 1)
    return (rows >= cols) & (same | (rows < TILE) | (cols >= TILE))


def attended_kernel(place, docs, q, k, v, state, out, far, up, own, down, turned):
    del place
    step = pl.program_id(0)
    same = docs[0, 0] == docs[0, 1]
    mask = causal(same)
    for head in range(state.shape[0]):
        cols = slice(head * HDIM, (head + 1) * HDIM)
        query = q[:, cols]
        attn = jnp.where(mask, SCALE * mul(query, k[:, cols], 1, 1), 0.0).astype(BF16)
        got = mul(attn, v[:, cols], 1, 0)
        got = got + mul(joined(query, same, False), (SCALE * state[head]).astype(BF16), 1, 0)
        got = got.astype(BF16)
        out[:, cols] = got
        turned[cols, :] = got.astype(F32).T

    for when, wide in enumerate((far, up, own, down)):

        @pl.when(step == when)
        def _(wide=wide):
            wide[...] = turned[...].astype(wide.dtype)


def grads_kernel(docs, q, k, v, g, state, rev, gq, gk, gv):
    same = docs[0, 0] == docs[0, 1]
    mask = causal(same)
    for head in range(state.shape[0]):
        cols = slice(head * HDIM, (head + 1) * HDIM)
        qh, kh, vh, gh = q[:, cols], k[:, cols], v[:, cols], g[:, cols]
        attn_q = jnp.where(mask, SCALE * mul(qh, kh, 1, 1), 0.0).astype(BF16)
        attn_g = jnp.where(mask, SCALE * mul(gh, vh, 1, 1), 0.0).astype(BF16)
        state_b = (SCALE * state[head]).astype(BF16)
        rev_b = (SCALE * rev[head]).astype(BF16)
        gq[:, cols] = (mul(attn_g, kh, 1, 0) + mul(joined(gh, same, False), state_b, 1, 1)).astype(BF16)
        gk[:, cols] = (mul(attn_g, qh, 0, 0) + mul(joined(vh, same, True), rev_b, 1, 0)).astype(BF16)
        gv[:, cols] = (mul(attn_q, gh, 0, 0) + mul(joined(kh, same, True), rev_b, 1, 1)).astype(BF16)


def pack_kernel(own, *rest):
    others, out = rest[:-1], rest[-1]
    out[:TOKENS] = own[...]
    start = TOKENS
    for other in others:
        out[start : start + other.shape[0]] = other[...].astype(BF16)
        start += other.shape[0]


def pack(own, others):
    width = own.shape[1]
    step = 4 * HDIM

    def cols(count):
        return pl.BlockSpec((count, step), lambda i: (0, i))

    return pl.pallas_call(
        pack_kernel,
        grid=(width // step,),
        in_specs=[cols(TOKENS)] + [cols(other.shape[0]) for other in others],
        out_specs=cols(4 * TOKENS),
        out_shape=jax.ShapeDtypeStruct((4 * TOKENS, width), BF16),
        compiler_params=params(SMALL),
        cost_estimate=cost(1 << 20, 12 << 20),
        name="pack",
    )(own, *others)


def product_kernel(side, att_own, att_low, att_high, att_far, gathered, out, left):
    del side

    @pl.when(pl.program_id(0) == 0)
    def _():
        for i, att in enumerate((att_own, att_low, att_high, att_far)):
            left[:, i * TOKENS : (i + 1) * TOKENS] = att[...].astype(BF16)

    total = mul(left[...], gathered[...], 1, 0)
    for block in range(out.shape[0]):
        out[block] = total[:, block * HDIM : (block + 1) * HDIM]


def product(atts, gathered, side):
    width = gathered.shape[1]
    step = 4 * HDIM
    rows = pl.BlockSpec((TOKENS, TOKENS), lambda i, w: (w[0], 0))
    spec = pltpu.PrefetchScalarGridSpec(
        num_scalar_prefetch=1,
        grid=(width // step,),
        in_specs=[rows] * 4 + [pl.BlockSpec((4 * TOKENS, step), lambda i, w: (0, i))],
        out_specs=pl.BlockSpec((step // HDIM, TOKENS, HDIM), lambda i, w: (i, 0, 0)),
        scratch_shapes=[pltpu.VMEM((TOKENS, 4 * TOKENS), BF16)],
    )
    return pl.pallas_call(
        product_kernel,
        grid_spec=spec,
        out_shape=jax.ShapeDtypeStruct((width // HDIM, TOKENS, HDIM), F32),
        compiler_params=params(SMALL),
        cost_estimate=cost(WEIGH * PRODUCT, WEIGH),
        name="product",
    )(side.astype(jnp.int32).reshape(1), *atts, gathered)


def ring(step):
    return [(i, (i + step) % 4) for i in range(4)]


def body(queries, keys, values, weight, grad_out, docs):
    ctx = ("x", "z")
    q, k, v, go = queries[0], keys[0], values[0], grad_out[0]
    width = q.shape[1]
    factor = 1.0 / float(TOKENS * 128) ** 0.5

    ends = (0, TILE - MIDDLE, TILE, TILE + MIDDLE, TOKENS)
    cuts = [go[i:j].astype(F32) for i, j in zip(ends[:-1], ends[1:])]
    top, bottom = go[:TILE].astype(F32), go[TILE:].astype(F32)
    top, bottom, cuts, k, v = lax.optimization_barrier((top, bottom, cuts, k, v))
    low_top = lax.ppermute(top, "y", ring(1))
    high_bottom = lax.ppermute(bottom, "y", ring(-1))
    low_middle = lax.ppermute(cuts[2], "y", ring(1))
    high_middle = lax.ppermute(cuts[1], "y", ring(-1))
    low_rest = lax.ppermute(cuts[3], "y", ring(1))
    high_rest = lax.ppermute(cuts[0], "y", ring(-1))

    per = 2
    block = pl.BlockSpec((TOKENS, per * HDIM), lambda i: (0, i))
    summed = pl.BlockSpec((per, ROWS, HDIM), lambda i: (i, 0, 0))
    matrix = pl.BlockSpec((per, HDIM, HDIM), lambda i: (i, 0, 0))
    tokens = jax.ShapeDtypeStruct((TOKENS, width), BF16)
    payload = jax.ShapeDtypeStruct((HEADS, ROWS, HDIM), F32)

    trailing = pl.pallas_call(
        trailing_kernel,
        grid=(HEADS // 4,),
        in_specs=[SMEM] + [pl.BlockSpec((TOKENS, 4 * HDIM), lambda i: (0, i))] * 2,
        out_specs=pl.BlockSpec((4, ROWS, HDIM), lambda i: (i, 0, 0)),
        out_shape=payload,
        compiler_params=params(),
        cost_estimate=cost(2 * 32 * 128**3, 3 << 20),
        name="trailing",
    )(docs, k, v)
    by_head = lax.all_to_all(trailing, ctx, 0, 0, tiled=True)

    g, leading = pl.pallas_call(
        leading_kernel,
        grid=(HEADS // per,),
        in_specs=[
            SMEM,
            whole((TOKENS, width)),
            pl.BlockSpec((per * HDIM, width), lambda i: (i, 0)),
            block,
        ],
        out_specs=[block, summed],
        out_shape=[tokens, payload],
        compiler_params=params(),
        cost_estimate=cost(2 * 256 * 2048 * 2048, 12 << 20),
        name="leading",
    )(docs, go, weight, q)

    def scan(reverse, *parts):
        return pl.pallas_call(
            functools.partial(scan_kernel, reverse),
            out_shape=jax.ShapeDtypeStruct((BLOCKS, HDIM + ROWS * (len(parts) - 1), HDIM), F32),
            compiler_params=params(SMALL),
            cost_estimate=cost(1 << 20, 2 << 20),
            name="scan",
        )(*parts)

    by_head, leading, low_top, high_bottom, low_middle, high_middle = lax.optimization_barrier(
        (by_head, leading, low_top, high_bottom, low_middle, high_middle)
    )
    far_top = lax.ppermute(low_top, "y", ring(1))
    far_bottom = lax.ppermute(high_bottom, "y", ring(-1))
    both = lax.all_to_all(scan(False, by_head, leading), ctx, 0, 0, tiled=True)

    def group(i, w):
        return (w[0] + 6 - i) % 4

    place = lax.axis_index("y").astype(jnp.int32).reshape(1)
    four = pl.BlockSpec((TOKENS, 4 * HDIM), lambda i, w: (0, group(i, w)))
    turned = jax.ShapeDtypeStruct((4 * HDIM, TOKENS), F32)
    attended, far, up, att_own, down = pl.pallas_call(
        attended_kernel,
        grid_spec=pltpu.PrefetchScalarGridSpec(
            num_scalar_prefetch=1,
            grid=(HEADS // 4,),
            in_specs=[SMEM, four, four, four, pl.BlockSpec((4, HDIM, HDIM), lambda i, w: (group(i, w), 0, 0))],
            out_specs=[four] + [pl.BlockSpec(part.shape, lambda i, w: (0, 0)) for part in (turned,) * 4],
            scratch_shapes=[pltpu.VMEM((4 * HDIM, TOKENS), F32)],
        ),
        out_shape=[tokens, turned, turned, jax.ShapeDtypeStruct(turned.shape, BF16), turned],
        compiler_params=params(SMALL),
        cost_estimate=cost(2 * 32 * 4 * 128**3, 7 << 20),
        name="attended",
    )(place, docs, q, k, v, both)
    behind, attended = lax.optimization_barrier((both, attended))
    rev_scan = scan(True, behind)
    rev = lax.all_to_all(rev_scan, ctx, 0, 0, tiled=True)
    far, up, down, far_top, far_bottom, low_rest, high_rest = lax.optimization_barrier(
        (far, up, down, far_top, far_bottom, low_rest, high_rest)
    )
    far = lax.ppermute(far, "y", ring(2))
    up = lax.ppermute(up, "y", ring(1))
    down = lax.ppermute(down, "y", ring(-1))
    gathered = pack(
        go, (low_top, low_middle, low_rest, high_rest, high_middle, high_bottom, far_top, far_bottom)
    )

    layer_out = jnp.dot(attended, weight, preferred_element_type=F32).astype(BF16)

    core = lax.axis_index("core")
    atts = (att_own, up, down, far)
    given = product(atts, gathered, 1 - core)
    core, rev = lax.optimization_barrier((core, rev))
    kept = product(atts, gathered, core)
    taken = lax.ppermute(given, "core", [(0, 1), (1, 0)])
    spread = lax.all_to_all((kept + taken) * factor, ctx, 0, 0, tiled=True)
    grad_weight = jnp.sum(spread, axis=0)

    grad_q, grad_k, grad_v = pl.pallas_call(
        grads_kernel,
        grid=(HEADS // per,),
        in_specs=[SMEM, block, block, block, block, matrix, matrix],
        out_specs=[block, block, block],
        out_shape=[tokens, tokens, tokens],
        compiler_params=params(),
        cost_estimate=cost(2 * 32 * 10 * 128**3, 9 << 20),
        name="grads",
    )(docs, q, k, v, g, both, rev)
    return layer_out[None], grad_q[None], grad_k[None], grad_v[None], grad_weight


def solution(mesh):
    fine = Mesh(mesh.devices.reshape(4, 2, 4, 4), ("y", "core", "x", "z"))
    dp, ctx = ("y", "core"), ("x", "z")
    tokens = P(dp, ctx, None)
    return jax.shard_map(
        body,
        mesh=fine,
        in_specs=(tokens, tokens, tokens, P(), tokens, P(dp, ctx)),
        out_specs=(tokens, tokens, tokens, tokens, P(dp, ctx)),
        check_vma=False,
    )
```

```python
import functools

import jax
import jax.numpy as jnp
from jax import lax
from jax.experimental import pallas as pl
from jax.experimental.pallas import tpu as pltpu
from jax.sharding import Mesh
from jax.sharding import PartitionSpec as P

HEADS = 16
HDIM = 128
TILE = 128
TOKENS = 2 * TILE
BLOCKS = 16
ROWS = HDIM + 8
SCALE = 1.0 / HDIM
F32 = jnp.float32
BF16 = jnp.bfloat16
VMEM = 60 * 1024 * 1024
SMALL = 24 * 1024 * 1024
WEIGH = 100
PRODUCT = 15 << 30


def mul(a, b, da, db):
    return lax.dot_general(a, b, (((da,), (db,)), ((), ())), preferred_element_type=F32)


def params(limit=VMEM):
    return pltpu.CompilerParams(vmem_limit_bytes=limit)


def cost(flops, moved):
    return pl.CostEstimate(flops=int(flops) // WEIGH, bytes_accessed=int(moved) // WEIGH, transcendentals=0)


def whole(shape):
    return pl.BlockSpec(shape, lambda *_: (0,) * len(shape))


SMEM = pl.BlockSpec(memory_space=pltpu.SMEM)


def put_ends(ref, head, docs):
    ref[head, HDIM : HDIM + 1, :] = jnp.full((1, HDIM), docs[0, 0], jnp.int32).astype(F32)
    ref[head, HDIM + 1 : HDIM + 2, :] = jnp.full((1, HDIM), docs[0, 1], jnp.int32).astype(F32)
    ref[head, HDIM + 2 :, :] = jnp.zeros((ROWS - HDIM - 2, HDIM), F32)


def joined(x, keep, first):
    rows = lax.broadcasted_iota(jnp.int32, x.shape, 0)
    return jnp.where(keep | ((rows >= TILE) if first else (rows < TILE)), x, jnp.zeros_like(x))


def trailing_kernel(docs, k, v, out):
    same = docs[0, 0] == docs[0, 1]
    for pair in range(out.shape[0] // 2):
        cols = slice(2 * pair * HDIM, 2 * (pair + 1) * HDIM)
        kv = mul(joined(k[:, cols], same, True), v[:, cols], 0, 0)
        for head in range(2):
            part = slice(head * HDIM, (head + 1) * HDIM)
            out[2 * pair + head, :HDIM, :] = kv[part, part]
            put_ends(out, 2 * pair + head, docs)


def leading_kernel(docs, grad_out, weight, q, g, out):
    grad = mul(grad_out[...], weight[...], 1, 1).astype(BF16)
    g[...] = grad
    qg = mul(joined(grad, docs[0, 0] == docs[0, 1], False), q[...], 0, 0)
    for head in range(2):
        part = slice(head * HDIM, (head + 1) * HDIM)
        out[head, :HDIM, :] = qg[part, part]
        put_ends(out, head, docs)


def scan_kernel(reverse, part, *rest):
    out = rest[-1]
    base = part.shape[1] - ROWS
    carried = jnp.zeros((HDIM, HDIM), F32)
    near = jnp.full((1, HDIM), -1.0, F32)
    order = range(BLOCKS - 1, -1, -1) if reverse else range(BLOCKS)
    for block in order:
        first = part[block, base + HDIM : base + HDIM + 1, :]
        last = part[block, base + HDIM + 1 : base + HDIM + 2, :]
        entry, leave = (last, first) if reverse else (first, last)
        state = jnp.where(near == entry, carried, 0.0)
        out[block, :HDIM, :] = state
        carried = part[block, base : base + HDIM, :] + jnp.where(first == last, state, 0.0)
        near = leave
    for along in rest[:-1]:
        out[:, HDIM:, :] = along[...]


def causal(same):
    rows = lax.broadcasted_iota(jnp.int32, (TOKENS, TOKENS), 0)
    cols = lax.broadcasted_iota(jnp.int32, (TOKENS, TOKENS), 1)
    return (rows >= cols) & (same | (rows < TILE) | (cols >= TILE))


def attended_kernel(place, docs, q, k, v, state, out, far, up, own, down, turned):
    del place
    step = pl.program_id(0)
    same = docs[0, 0] == docs[0, 1]
    mask = causal(same)
    for head in range(state.shape[0]):
        cols = slice(head * HDIM, (head + 1) * HDIM)
        query = q[:, cols]
        attn = jnp.where(mask, SCALE * mul(query, k[:, cols], 1, 1), 0.0).astype(BF16)
        got = mul(attn, v[:, cols], 1, 0)
        got = got + mul(joined(query, same, False), (SCALE * state[head]).astype(BF16), 1, 0)
        got = got.astype(BF16)
        out[:, cols] = got
        turned[cols, :] = got.astype(F32).T

    for when, wide in enumerate((far, up, own, down)):

        @pl.when(step == when)
        def _(wide=wide):
            wide[...] = turned[...].astype(wide.dtype)


def grads_kernel(docs, q, k, v, g, state, rev, gq, gk, gv):
    same = docs[0, 0] == docs[0, 1]
    mask = causal(same)
    for head in range(state.shape[0]):
        cols = slice(head * HDIM, (head + 1) * HDIM)
        qh, kh, vh, gh = q[:, cols], k[:, cols], v[:, cols], g[:, cols]
        attn_q = jnp.where(mask, SCALE * mul(qh, kh, 1, 1), 0.0).astype(BF16)
        attn_g = jnp.where(mask, SCALE * mul(gh, vh, 1, 1), 0.0).astype(BF16)
        state_b = (SCALE * state[head]).astype(BF16)
        rev_b = (SCALE * rev[head]).astype(BF16)
        gq[:, cols] = (mul(attn_g, kh, 1, 0) + mul(joined(gh, same, False), state_b, 1, 1)).astype(BF16)
        gk[:, cols] = (mul(attn_g, qh, 0, 0) + mul(joined(vh, same, True), rev_b, 1, 0)).astype(BF16)
        gv[:, cols] = (mul(attn_q, gh, 0, 0) + mul(joined(kh, same, True), rev_b, 1, 1)).astype(BF16)


def pack_kernel(own, *rest):
    others, out = rest[:-1], rest[-1]
    out[:TOKENS] = own[...]
    start = TOKENS
    for other in others:
        out[start : start + other.shape[0]] = other[...].astype(BF16)
        start += other.shape[0]


def pack(own, others):
    width = own.shape[1]
    step = 4 * HDIM

    def cols(count):
        return pl.BlockSpec((count, step), lambda i: (0, i))

    return pl.pallas_call(
        pack_kernel,
        grid=(width // step,),
        in_specs=[cols(TOKENS)] + [cols(other.shape[0]) for other in others],
        out_specs=cols(4 * TOKENS),
        out_shape=jax.ShapeDtypeStruct((4 * TOKENS, width), BF16),
        compiler_params=params(SMALL),
        cost_estimate=cost(1 << 20, 12 << 20),
        name="pack",
    )(own, *others)


def product_kernel(side, att_own, att_low, att_high, att_far, gathered, out, left):
    del side

    @pl.when(pl.program_id(0) == 0)
    def _():
        for i, att in enumerate((att_own, att_low, att_high, att_far)):
            left[:, i * TOKENS : (i + 1) * TOKENS] = att[...].astype(BF16)

    total = mul(left[...], gathered[...], 1, 0)
    for block in range(out.shape[0]):
        out[block] = total[:, block * HDIM : (block + 1) * HDIM]


def product(atts, gathered, side):
    width = gathered.shape[1]
    step = 4 * HDIM
    rows = pl.BlockSpec((TOKENS, TOKENS), lambda i, w: (w[0], 0))
    spec = pltpu.PrefetchScalarGridSpec(
        num_scalar_prefetch=1,
        grid=(width // step,),
        in_specs=[rows] * 4 + [pl.BlockSpec((4 * TOKENS, step), lambda i, w: (0, i))],
        out_specs=pl.BlockSpec((step // HDIM, TOKENS, HDIM), lambda i, w: (i, 0, 0)),
        scratch_shapes=[pltpu.VMEM((TOKENS, 4 * TOKENS), BF16)],
    )
    return pl.pallas_call(
        product_kernel,
        grid_spec=spec,
        out_shape=jax.ShapeDtypeStruct((width // HDIM, TOKENS, HDIM), F32),
        compiler_params=params(SMALL),
        cost_estimate=cost(WEIGH * PRODUCT, WEIGH),
        name="product",
    )(side.astype(jnp.int32).reshape(1), *atts, gathered)


def ring(step):
    return [(i, (i + step) % 4) for i in range(4)]


def body(queries, keys, values, weight, grad_out, docs):
    ctx = ("x", "z")
    q, k, v, go = queries[0], keys[0], values[0], grad_out[0]
    width = q.shape[1]
    factor = 1.0 / float(TOKENS * 128) ** 0.5

    top, bottom = go[:TILE].astype(F32), go[TILE:].astype(F32)
    top, bottom, k, v = lax.optimization_barrier((top, bottom, k, v))
    low_top = lax.ppermute(top, "y", ring(1))
    high_bottom = lax.ppermute(bottom, "y", ring(-1))

    per = 2
    block = pl.BlockSpec((TOKENS, per * HDIM), lambda i: (0, i))
    summed = pl.BlockSpec((per, ROWS, HDIM), lambda i: (i, 0, 0))
    matrix = pl.BlockSpec((per, HDIM, HDIM), lambda i: (i, 0, 0))
    tokens = jax.ShapeDtypeStruct((TOKENS, width), BF16)
    payload = jax.ShapeDtypeStruct((HEADS, ROWS, HDIM), F32)

    trailing = pl.pallas_call(
        trailing_kernel,
        grid=(HEADS // 4,),
        in_specs=[SMEM] + [pl.BlockSpec((TOKENS, 4 * HDIM), lambda i: (0, i))] * 2,
        out_specs=pl.BlockSpec((4, ROWS, HDIM), lambda i: (i, 0, 0)),
        out_shape=payload,
        compiler_params=params(),
        cost_estimate=cost(2 * 32 * 128**3, 3 << 20),
        name="trailing",
    )(docs, k, v)
    by_head = lax.all_to_all(trailing, ctx, 0, 0, tiled=True)

    low_bottom = lax.ppermute(bottom, "y", ring(1))
    high_top = lax.ppermute(top, "y", ring(-1))

    g, leading = pl.pallas_call(
        leading_kernel,
        grid=(HEADS // per,),
        in_specs=[
            SMEM,
            whole((TOKENS, width)),
            pl.BlockSpec((per * HDIM, width), lambda i: (i, 0)),
            block,
        ],
        out_specs=[block, summed],
        out_shape=[tokens, payload],
        compiler_params=params(),
        cost_estimate=cost(2 * 256 * 2048 * 2048, 12 << 20),
        name="leading",
    )(docs, go, weight, q)

    def scan(reverse, *parts):
        return pl.pallas_call(
            functools.partial(scan_kernel, reverse),
            out_shape=jax.ShapeDtypeStruct((BLOCKS, HDIM + ROWS * (len(parts) - 1), HDIM), F32),
            compiler_params=params(SMALL),
            cost_estimate=cost(1 << 20, 2 << 20),
            name="scan",
        )(*parts)

    by_head, leading, low_top, high_bottom = lax.optimization_barrier((by_head, leading, low_top, high_bottom))
    far_top = lax.ppermute(low_top, "y", ring(1))
    far_bottom = lax.ppermute(high_bottom, "y", ring(-1))
    state = lax.all_to_all(scan(False, by_head), ctx, 0, 0, tiled=True)
    leading, state, low_bottom, high_top = lax.optimization_barrier((leading, state, low_bottom, high_top))
    rev_by_head = lax.all_to_all(leading, ctx, 0, 0, tiled=True)

    def group(i, w):
        return (w[0] + 6 - i) % 4

    place = lax.axis_index("y").astype(jnp.int32).reshape(1)
    four = pl.BlockSpec((TOKENS, 4 * HDIM), lambda i, w: (0, group(i, w)))
    turned = jax.ShapeDtypeStruct((4 * HDIM, TOKENS), F32)
    attended, far, up, att_own, down = pl.pallas_call(
        attended_kernel,
        grid_spec=pltpu.PrefetchScalarGridSpec(
            num_scalar_prefetch=1,
            grid=(HEADS // 4,),
            in_specs=[SMEM, four, four, four, pl.BlockSpec((4, HDIM, HDIM), lambda i, w: (group(i, w), 0, 0))],
            out_specs=[four] + [pl.BlockSpec(part.shape, lambda i, w: (0, 0)) for part in (turned,) * 4],
            scratch_shapes=[pltpu.VMEM((4 * HDIM, TOKENS), F32)],
        ),
        out_shape=[tokens, turned, turned, jax.ShapeDtypeStruct(turned.shape, BF16), turned],
        compiler_params=params(SMALL),
        cost_estimate=cost(2 * 32 * 4 * 128**3, 7 << 20),
        name="attended",
    )(place, docs, q, k, v, state)
    rev_scan = scan(True, rev_by_head)
    far, up, down, far_top, far_bottom = lax.optimization_barrier((far, up, down, far_top, far_bottom))
    far = lax.ppermute(far, "y", ring(2))
    up = lax.ppermute(up, "y", ring(1))
    down = lax.ppermute(down, "y", ring(-1))
    gathered = pack(
        go, (low_top, low_bottom, high_top, high_bottom, far_top, far_bottom)
    )

    layer_out = jnp.dot(attended, weight, preferred_element_type=F32).astype(BF16)

    core = lax.axis_index("core")
    gathered, rev_scan = lax.optimization_barrier((gathered, rev_scan))
    rev = lax.all_to_all(rev_scan, ctx, 0, 0, tiled=True)
    atts = (att_own, up, down, far)
    given = product(atts, gathered, 1 - core)
    core, rev = lax.optimization_barrier((core, rev))
    kept = product(atts, gathered, core)
    taken = lax.ppermute(given, "core", [(0, 1), (1, 0)])
    spread = lax.all_to_all((kept + taken) * factor, ctx, 0, 0, tiled=True)
    grad_weight = jnp.sum(spread, axis=0)

    grad_q, grad_k, grad_v = pl.pallas_call(
        grads_kernel,
        grid=(HEADS // per,),
        in_specs=[SMEM, block, block, block, block, matrix, matrix],
        out_specs=[block, block, block],
        out_shape=[tokens, tokens, tokens],
        compiler_params=params(SMALL),
        cost_estimate=cost(2 * 32 * 10 * 128**3, 9 << 20),
        name="grads",
    )(docs, q, k, v, g, state, rev)
    return layer_out[None], grad_q[None], grad_k[None], grad_v[None], grad_weight


def solution(mesh):
    fine = Mesh(mesh.devices.reshape(4, 2, 4, 4), ("y", "core", "x", "z"))
    dp, ctx = ("y", "core"), ("x", "z")
    tokens = P(dp, ctx, None)
    return jax.shard_map(
        body,
        mesh=fine,
        in_specs=(tokens, tokens, tokens, P(), tokens, P(dp, ctx)),
        out_specs=(tokens, tokens, tokens, tokens, P(dp, ctx)),
        check_vma=False,
    )
```

```python
import functools

import jax
import jax.numpy as jnp
from jax import lax
from jax.experimental import pallas as pl
from jax.experimental.pallas import tpu as pltpu
from jax.sharding import Mesh
from jax.sharding import PartitionSpec as P

HEADS = 16
HDIM = 128
TILE = 128
TOKENS = 2 * TILE
BLOCKS = 16
ROWS = HDIM + 8
SCALE = 1.0 / HDIM
F32 = jnp.float32
BF16 = jnp.bfloat16
VMEM = 60 * 1024 * 1024
SMALL = 24 * 1024 * 1024
WEIGH = 100
PRODUCT = 15 << 30


def mul(a, b, da, db):
    return lax.dot_general(a, b, (((da,), (db,)), ((), ())), preferred_element_type=F32)


def params(limit=VMEM):
    return pltpu.CompilerParams(vmem_limit_bytes=limit)


def cost(flops, moved):
    return pl.CostEstimate(flops=int(flops) // WEIGH, bytes_accessed=int(moved) // WEIGH, transcendentals=0)


def whole(shape):
    return pl.BlockSpec(shape, lambda *_: (0,) * len(shape))


SMEM = pl.BlockSpec(memory_space=pltpu.SMEM)


def put_ends(ref, head, docs):
    ref[head, HDIM : HDIM + 1, :] = jnp.full((1, HDIM), docs[0, 0], jnp.int32).astype(F32)
    ref[head, HDIM + 1 : HDIM + 2, :] = jnp.full((1, HDIM), docs[0, 1], jnp.int32).astype(F32)
    ref[head, HDIM + 2 :, :] = jnp.zeros((ROWS - HDIM - 2, HDIM), F32)


def joined(x, keep, first):
    rows = lax.broadcasted_iota(jnp.int32, x.shape, 0)
    return jnp.where(keep | ((rows >= TILE) if first else (rows < TILE)), x, jnp.zeros_like(x))


def trailing_kernel(docs, k, v, out):
    same = docs[0, 0] == docs[0, 1]
    for pair in range(out.shape[0] // 2):
        cols = slice(2 * pair * HDIM, 2 * (pair + 1) * HDIM)
        kv = mul(joined(k[:, cols], same, True), v[:, cols], 0, 0)
        for head in range(2):
            part = slice(head * HDIM, (head + 1) * HDIM)
            out[2 * pair + head, :HDIM, :] = kv[part, part]
            put_ends(out, 2 * pair + head, docs)


def leading_kernel(docs, grad_out, weight, q, g, out):
    grad = mul(grad_out[...], weight[...], 1, 1).astype(BF16)
    g[...] = grad
    qg = mul(joined(grad, docs[0, 0] == docs[0, 1], False), q[...], 0, 0)
    for head in range(2):
        part = slice(head * HDIM, (head + 1) * HDIM)
        out[head, :HDIM, :] = qg[part, part]
        put_ends(out, head, docs)


def scan_kernel(reverse, part, *rest):
    out = rest[-1]
    base = part.shape[1] - ROWS
    carried = jnp.zeros((HDIM, HDIM), F32)
    near = jnp.full((1, HDIM), -1.0, F32)
    order = range(BLOCKS - 1, -1, -1) if reverse else range(BLOCKS)
    for block in order:
        first = part[block, base + HDIM : base + HDIM + 1, :]
        last = part[block, base + HDIM + 1 : base + HDIM + 2, :]
        entry, leave = (last, first) if reverse else (first, last)
        state = jnp.where(near == entry, carried, 0.0)
        out[block, :HDIM, :] = state
        carried = part[block, base : base + HDIM, :] + jnp.where(first == last, state, 0.0)
        near = leave
    for along in rest[:-1]:
        out[:, HDIM:, :] = along[...]


def causal(same):
    rows = lax.broadcasted_iota(jnp.int32, (TOKENS, TOKENS), 0)
    cols = lax.broadcasted_iota(jnp.int32, (TOKENS, TOKENS), 1)
    return (rows >= cols) & (same | (rows < TILE) | (cols >= TILE))


def attended_kernel(place, docs, q, k, v, state, out, far, up, own, down, turned):
    del place
    step = pl.program_id(0)
    same = docs[0, 0] == docs[0, 1]
    mask = causal(same)
    for head in range(state.shape[0]):
        cols = slice(head * HDIM, (head + 1) * HDIM)
        query = q[:, cols]
        attn = jnp.where(mask, SCALE * mul(query, k[:, cols], 1, 1), 0.0).astype(BF16)
        got = mul(attn, v[:, cols], 1, 0)
        got = got + mul(joined(query, same, False), (SCALE * state[head]).astype(BF16), 1, 0)
        got = got.astype(BF16)
        out[:, cols] = got
        turned[cols, :] = got.astype(F32).T

    for when, wide in enumerate((far, up, own, down)):

        @pl.when(step == when)
        def _(wide=wide):
            wide[...] = turned[...].astype(wide.dtype)


def grads_kernel(docs, q, k, v, g, state, rev, gq, gk, gv):
    same = docs[0, 0] == docs[0, 1]
    mask = causal(same)
    for head in range(state.shape[0]):
        cols = slice(head * HDIM, (head + 1) * HDIM)
        qh, kh, vh, gh = q[:, cols], k[:, cols], v[:, cols], g[:, cols]
        attn_q = jnp.where(mask, SCALE * mul(qh, kh, 1, 1), 0.0).astype(BF16)
        attn_g = jnp.where(mask, SCALE * mul(gh, vh, 1, 1), 0.0).astype(BF16)
        state_b = (SCALE * state[head]).astype(BF16)
        rev_b = (SCALE * rev[head]).astype(BF16)
        gq[:, cols] = (mul(attn_g, kh, 1, 0) + mul(joined(gh, same, False), state_b, 1, 1)).astype(BF16)
        gk[:, cols] = (mul(attn_g, qh, 0, 0) + mul(joined(vh, same, True), rev_b, 1, 0)).astype(BF16)
        gv[:, cols] = (mul(attn_q, gh, 0, 0) + mul(joined(kh, same, True), rev_b, 1, 1)).astype(BF16)


def pack_kernel(own, *rest):
    others, out = rest[:-1], rest[-1]
    out[:TOKENS] = own[...]
    start = TOKENS
    for other in others:
        out[start : start + other.shape[0]] = other[...].astype(BF16)
        start += other.shape[0]


def pack(own, others):
    width = own.shape[1]
    step = 4 * HDIM

    def cols(count):
        return pl.BlockSpec((count, step), lambda i: (0, i))

    return pl.pallas_call(
        pack_kernel,
        grid=(width // step,),
        in_specs=[cols(TOKENS)] + [cols(other.shape[0]) for other in others],
        out_specs=cols(4 * TOKENS),
        out_shape=jax.ShapeDtypeStruct((4 * TOKENS, width), BF16),
        compiler_params=params(),
        cost_estimate=cost(1 << 20, 12 << 20),
        name="pack",
    )(own, *others)


def product_kernel(side, att_own, att_low, att_high, att_far, gathered, out, left):
    del side

    @pl.when(pl.program_id(0) == 0)
    def _():
        for i, att in enumerate((att_own, att_low, att_high, att_far)):
            left[:, i * TOKENS : (i + 1) * TOKENS] = att[...].astype(BF16)

    total = mul(left[...], gathered[...], 1, 0)
    for block in range(out.shape[0]):
        out[block] = total[:, block * HDIM : (block + 1) * HDIM]


def product(atts, gathered, side):
    width = gathered.shape[1]
    step = 4 * HDIM
    rows = pl.BlockSpec((TOKENS, TOKENS), lambda i, w: (w[0], 0))
    spec = pltpu.PrefetchScalarGridSpec(
        num_scalar_prefetch=1,
        grid=(width // step,),
        in_specs=[rows] * 4 + [pl.BlockSpec((4 * TOKENS, step), lambda i, w: (0, i))],
        out_specs=pl.BlockSpec((step // HDIM, TOKENS, HDIM), lambda i, w: (i, 0, 0)),
        scratch_shapes=[pltpu.VMEM((TOKENS, 4 * TOKENS), BF16)],
    )
    return pl.pallas_call(
        product_kernel,
        grid_spec=spec,
        out_shape=jax.ShapeDtypeStruct((width // HDIM, TOKENS, HDIM), F32),
        compiler_params=params(),
        cost_estimate=cost(WEIGH * PRODUCT, WEIGH),
        name="product",
    )(side.astype(jnp.int32).reshape(1), *atts, gathered)


def ring(step):
    return [(i, (i + step) % 4) for i in range(4)]


def body(queries, keys, values, weight, grad_out, docs):
    ctx = ("x", "z")
    q, k, v, go = queries[0], keys[0], values[0], grad_out[0]
    width = q.shape[1]
    factor = 1.0 / float(TOKENS * 128) ** 0.5

    top, bottom = go[:TILE].astype(F32), go[TILE:].astype(F32)
    top, bottom, k, v = lax.optimization_barrier((top, bottom, k, v))
    low_top = lax.ppermute(top, "y", ring(1))
    high_bottom = lax.ppermute(bottom, "y", ring(-1))

    per = 2
    block = pl.BlockSpec((TOKENS, per * HDIM), lambda i: (0, i))
    summed = pl.BlockSpec((per, ROWS, HDIM), lambda i: (i, 0, 0))
    matrix = pl.BlockSpec((per, HDIM, HDIM), lambda i: (i, 0, 0))
    tokens = jax.ShapeDtypeStruct((TOKENS, width), BF16)
    payload = jax.ShapeDtypeStruct((HEADS, ROWS, HDIM), F32)

    trailing = pl.pallas_call(
        trailing_kernel,
        grid=(HEADS // 4,),
        in_specs=[SMEM] + [pl.BlockSpec((TOKENS, 4 * HDIM), lambda i: (0, i))] * 2,
        out_specs=pl.BlockSpec((4, ROWS, HDIM), lambda i: (i, 0, 0)),
        out_shape=payload,
        compiler_params=params(),
        cost_estimate=cost(2 * 32 * 128**3, 3 << 20),
        name="trailing",
    )(docs, k, v)
    by_head = lax.all_to_all(trailing, ctx, 0, 0, tiled=True)

    low_bottom = lax.ppermute(bottom, "y", ring(1))
    high_top = lax.ppermute(top, "y", ring(-1))

    g, leading = pl.pallas_call(
        leading_kernel,
        grid=(HEADS // per,),
        in_specs=[
            SMEM,
            whole((TOKENS, width)),
            pl.BlockSpec((per * HDIM, width), lambda i: (i, 0)),
            block,
        ],
        out_specs=[block, summed],
        out_shape=[tokens, payload],
        compiler_params=params(),
        cost_estimate=cost(2 * 256 * 2048 * 2048, 12 << 20),
        name="leading",
    )(docs, go, weight, q)

    def scan(reverse, *parts):
        return pl.pallas_call(
            functools.partial(scan_kernel, reverse),
            out_shape=jax.ShapeDtypeStruct((BLOCKS, HDIM + ROWS * (len(parts) - 1), HDIM), F32),
            compiler_params=params(SMALL),
            cost_estimate=cost(1 << 20, 2 << 20),
            name="scan",
        )(*parts)

    by_head, leading, low_top, high_bottom = lax.optimization_barrier((by_head, leading, low_top, high_bottom))
    far_top = lax.ppermute(low_top, "y", ring(1))
    far_bottom = lax.ppermute(high_bottom, "y", ring(-1))
    state = lax.all_to_all(scan(False, by_head), ctx, 0, 0, tiled=True)
    leading, state, low_bottom, high_top = lax.optimization_barrier((leading, state, low_bottom, high_top))
    rev_by_head = lax.all_to_all(leading, ctx, 0, 0, tiled=True)

    def group(i, w):
        return (w[0] + 6 - i) % 4

    place = lax.axis_index("y").astype(jnp.int32).reshape(1)
    four = pl.BlockSpec((TOKENS, 4 * HDIM), lambda i, w: (0, group(i, w)))
    turned = jax.ShapeDtypeStruct((4 * HDIM, TOKENS), F32)
    attended, far, up, att_own, down = pl.pallas_call(
        attended_kernel,
        grid_spec=pltpu.PrefetchScalarGridSpec(
            num_scalar_prefetch=1,
            grid=(HEADS // 4,),
            in_specs=[SMEM, four, four, four, pl.BlockSpec((4, HDIM, HDIM), lambda i, w: (group(i, w), 0, 0))],
            out_specs=[four] + [pl.BlockSpec(part.shape, lambda i, w: (0, 0)) for part in (turned,) * 4],
            scratch_shapes=[pltpu.VMEM((4 * HDIM, TOKENS), F32)],
        ),
        out_shape=[tokens, turned, turned, jax.ShapeDtypeStruct(turned.shape, BF16), turned],
        compiler_params=params(SMALL),
        cost_estimate=cost(2 * 32 * 4 * 128**3, 7 << 20),
        name="attended",
    )(place, docs, q, k, v, state)
    rev_scan = scan(True, rev_by_head)
    far, up, down, far_top, far_bottom = lax.optimization_barrier((far, up, down, far_top, far_bottom))
    far = lax.ppermute(far, "y", ring(2))
    up = lax.ppermute(up, "y", ring(1))
    down = lax.ppermute(down, "y", ring(-1))
    far_top, rev_scan = lax.optimization_barrier((far_top, rev_scan))
    gathered = pack(
        go, (low_top, low_bottom, high_top, high_bottom, far_top, far_bottom)
    )

    layer_out = jnp.dot(attended, weight, preferred_element_type=F32).astype(BF16)

    core = lax.axis_index("core")
    rev = lax.all_to_all(rev_scan, ctx, 0, 0, tiled=True)
    atts = (att_own, up, down, far)
    given = product(atts, gathered, 1 - core)
    core, rev = lax.optimization_barrier((core, rev))
    kept = product(atts, gathered, core)
    taken = lax.ppermute(given, "core", [(0, 1), (1, 0)])
    spread = lax.all_to_all((kept + taken) * factor, ctx, 0, 0, tiled=True)
    grad_weight = jnp.sum(spread, axis=0)

    grad_q, grad_k, grad_v = pl.pallas_call(
        grads_kernel,
        grid=(HEADS // per,),
        in_specs=[SMEM, block, block, block, block, matrix, matrix],
        out_specs=[block, block, block],
        out_shape=[tokens, tokens, tokens],
        compiler_params=params(SMALL),
        cost_estimate=cost(2 * 32 * 10 * 128**3, 9 << 20),
        name="grads",
    )(docs, q, k, v, g, state, rev)
    return layer_out[None], grad_q[None], grad_k[None], grad_v[None], grad_weight


def solution(mesh):
    fine = Mesh(mesh.devices.reshape(4, 2, 4, 4), ("y", "core", "x", "z"))
    dp, ctx = ("y", "core"), ("x", "z")
    tokens = P(dp, ctx, None)
    return jax.shard_map(
        body,
        mesh=fine,
        in_specs=(tokens, tokens, tokens, P(), tokens, P(dp, ctx)),
        out_specs=(tokens, tokens, tokens, tokens, P(dp, ctx)),
        check_vma=False,
    )
```

```python
import functools

import jax
import jax.numpy as jnp
from jax import lax
from jax.experimental import pallas as pl
from jax.experimental.pallas import tpu as pltpu
from jax.sharding import Mesh
from jax.sharding import PartitionSpec as P

HEADS = 16
HDIM = 128
TILE = 128
TOKENS = 2 * TILE
BLOCKS = 16
ROWS = HDIM + 8
SCALE = 1.0 / HDIM
F32 = jnp.float32
BF16 = jnp.bfloat16
VMEM = 60 * 1024 * 1024
SMALL = 24 * 1024 * 1024
WEIGH = 100
PRODUCT = 15 << 30


def mul(a, b, da, db):
    return lax.dot_general(a, b, (((da,), (db,)), ((), ())), preferred_element_type=F32)


def params(limit=VMEM):
    return pltpu.CompilerParams(vmem_limit_bytes=limit)


def cost(flops, moved):
    return pl.CostEstimate(flops=int(flops) // WEIGH, bytes_accessed=int(moved) // WEIGH, transcendentals=0)


def whole(shape):
    return pl.BlockSpec(shape, lambda *_: (0,) * len(shape))


SMEM = pl.BlockSpec(memory_space=pltpu.SMEM)


def put_ends(ref, head, docs):
    ref[head, HDIM : HDIM + 1, :] = jnp.full((1, HDIM), docs[0, 0], jnp.int32).astype(F32)
    ref[head, HDIM + 1 : HDIM + 2, :] = jnp.full((1, HDIM), docs[0, 1], jnp.int32).astype(F32)
    ref[head, HDIM + 2 :, :] = jnp.zeros((ROWS - HDIM - 2, HDIM), F32)


def joined(x, keep, first):
    rows = lax.broadcasted_iota(jnp.int32, x.shape, 0)
    return jnp.where(keep | ((rows >= TILE) if first else (rows < TILE)), x, jnp.zeros_like(x))


def trailing_kernel(docs, k, v, out):
    same = docs[0, 0] == docs[0, 1]
    for pair in range(out.shape[0] // 2):
        cols = slice(2 * pair * HDIM, 2 * (pair + 1) * HDIM)
        kv = mul(joined(k[:, cols], same, True), v[:, cols], 0, 0)
        for head in range(2):
            part = slice(head * HDIM, (head + 1) * HDIM)
            out[2 * pair + head, :HDIM, :] = kv[part, part]
            put_ends(out, 2 * pair + head, docs)


def leading_kernel(docs, grad_out, weight, q, g, out):
    grad = mul(grad_out[...], weight[...], 1, 1).astype(BF16)
    g[...] = grad
    qg = mul(joined(grad, docs[0, 0] == docs[0, 1], False), q[...], 0, 0)
    for head in range(2):
        part = slice(head * HDIM, (head + 1) * HDIM)
        out[head, :HDIM, :] = qg[part, part]
        put_ends(out, head, docs)


def scan_kernel(reverse, part, *rest):
    out = rest[-1]
    base = part.shape[1] - ROWS
    carried = jnp.zeros((HDIM, HDIM), F32)
    near = jnp.full((1, HDIM), -1.0, F32)
    order = range(BLOCKS - 1, -1, -1) if reverse else range(BLOCKS)
    for block in order:
        first = part[block, base + HDIM : base + HDIM + 1, :]
        last = part[block, base + HDIM + 1 : base + HDIM + 2, :]
        entry, leave = (last, first) if reverse else (first, last)
        state = jnp.where(near == entry, carried, 0.0)
        out[block, :HDIM, :] = state
        carried = part[block, base : base + HDIM, :] + jnp.where(first == last, state, 0.0)
        near = leave
    for along in rest[:-1]:
        out[:, HDIM:, :] = along[...]


def causal(same):
    rows = lax.broadcasted_iota(jnp.int32, (TOKENS, TOKENS), 0)
    cols = lax.broadcasted_iota(jnp.int32, (TOKENS, TOKENS), 1)
    return (rows >= cols) & (same | (rows < TILE) | (cols >= TILE))


def attended_kernel(place, docs, q, k, v, state, out, far, up, own, down, turned):
    del place
    step = pl.program_id(0)
    same = docs[0, 0] == docs[0, 1]
    mask = causal(same)
    for head in range(state.shape[0]):
        cols = slice(head * HDIM, (head + 1) * HDIM)
        query = q[:, cols]
        attn = jnp.where(mask, SCALE * mul(query, k[:, cols], 1, 1), 0.0).astype(BF16)
        got = mul(attn, v[:, cols], 1, 0)
        got = got + mul(joined(query, same, False), (SCALE * state[head]).astype(BF16), 1, 0)
        got = got.astype(BF16)
        out[:, cols] = got
        turned[cols, :] = got.astype(F32).T

    for when, wide in enumerate((far, up, own, down)):

        @pl.when(step == when)
        def _(wide=wide):
            wide[...] = turned[...].astype(wide.dtype)


def grads_kernel(docs, q, k, v, g, state, rev, gq, gk, gv):
    same = docs[0, 0] == docs[0, 1]
    mask = causal(same)
    for head in range(state.shape[0]):
        cols = slice(head * HDIM, (head + 1) * HDIM)
        qh, kh, vh, gh = q[:, cols], k[:, cols], v[:, cols], g[:, cols]
        attn_q = jnp.where(mask, SCALE * mul(qh, kh, 1, 1), 0.0).astype(BF16)
        attn_g = jnp.where(mask, SCALE * mul(gh, vh, 1, 1), 0.0).astype(BF16)
        state_b = (SCALE * state[head]).astype(BF16)
        rev_b = (SCALE * rev[head]).astype(BF16)
        gq[:, cols] = (mul(attn_g, kh, 1, 0) + mul(joined(gh, same, False), state_b, 1, 1)).astype(BF16)
        gk[:, cols] = (mul(attn_g, qh, 0, 0) + mul(joined(vh, same, True), rev_b, 1, 0)).astype(BF16)
        gv[:, cols] = (mul(attn_q, gh, 0, 0) + mul(joined(kh, same, True), rev_b, 1, 1)).astype(BF16)


def pack_kernel(own, *rest):
    others, out = rest[:-1], rest[-1]
    out[:TOKENS] = own[...]
    start = TOKENS
    for other in others:
        out[start : start + other.shape[0]] = other[...].astype(BF16)
        start += other.shape[0]


def pack(own, others):
    width = own.shape[1]
    step = 4 * HDIM

    def cols(count):
        return pl.BlockSpec((count, step), lambda i: (0, i))

    return pl.pallas_call(
        pack_kernel,
        grid=(width // step,),
        in_specs=[cols(TOKENS)] + [cols(other.shape[0]) for other in others],
        out_specs=cols(4 * TOKENS),
        out_shape=jax.ShapeDtypeStruct((4 * TOKENS, width), BF16),
        compiler_params=params(SMALL),
        cost_estimate=cost(1 << 20, 12 << 20),
        name="pack",
    )(own, *others)


def product_kernel(side, att_own, att_low, att_high, att_far, gathered, out, left):
    del side

    @pl.when(pl.program_id(0) == 0)
    def _():
        for i, att in enumerate((att_own, att_low, att_high, att_far)):
            left[:, i * TOKENS : (i + 1) * TOKENS] = att[...].astype(BF16)

    total = mul(left[...], gathered[...], 1, 0)
    for block in range(out.shape[0]):
        out[block] = total[:, block * HDIM : (block + 1) * HDIM]


def product(atts, gathered, side):
    width = gathered.shape[1]
    step = 4 * HDIM
    rows = pl.BlockSpec((TOKENS, TOKENS), lambda i, w: (w[0], 0))
    spec = pltpu.PrefetchScalarGridSpec(
        num_scalar_prefetch=1,
        grid=(width // step,),
        in_specs=[rows] * 4 + [pl.BlockSpec((4 * TOKENS, step), lambda i, w: (0, i))],
        out_specs=pl.BlockSpec((step // HDIM, TOKENS, HDIM), lambda i, w: (i, 0, 0)),
        scratch_shapes=[pltpu.VMEM((TOKENS, 4 * TOKENS), BF16)],
    )
    return pl.pallas_call(
        product_kernel,
        grid_spec=spec,
        out_shape=jax.ShapeDtypeStruct((width // HDIM, TOKENS, HDIM), F32),
        compiler_params=params(SMALL),
        cost_estimate=cost(WEIGH * PRODUCT, WEIGH),
        name="product",
    )(side.astype(jnp.int32).reshape(1), *atts, gathered)


def ring(step):
    return [(i, (i + step) % 4) for i in range(4)]


def body(queries, keys, values, weight, grad_out, docs):
    ctx = ("x", "z")
    q, k, v, go = queries[0], keys[0], values[0], grad_out[0]
    width = q.shape[1]
    factor = 1.0 / float(TOKENS * 128) ** 0.5

    top, bottom = go[:TILE].astype(F32), go[TILE:].astype(F32)
    top, bottom, k, v = lax.optimization_barrier((top, bottom, k, v))
    low_top = lax.ppermute(top, "y", ring(1))
    high_bottom = lax.ppermute(bottom, "y", ring(-1))

    per = 2
    block = pl.BlockSpec((TOKENS, per * HDIM), lambda i: (0, i))
    summed = pl.BlockSpec((per, ROWS, HDIM), lambda i: (i, 0, 0))
    matrix = pl.BlockSpec((per, HDIM, HDIM), lambda i: (i, 0, 0))
    tokens = jax.ShapeDtypeStruct((TOKENS, width), BF16)
    payload = jax.ShapeDtypeStruct((HEADS, ROWS, HDIM), F32)

    trailing = pl.pallas_call(
        trailing_kernel,
        grid=(HEADS // 4,),
        in_specs=[SMEM] + [pl.BlockSpec((TOKENS, 4 * HDIM), lambda i: (0, i))] * 2,
        out_specs=pl.BlockSpec((4, ROWS, HDIM), lambda i: (i, 0, 0)),
        out_shape=payload,
        compiler_params=params(),
        cost_estimate=cost(2 * 32 * 128**3, 3 << 20),
        name="trailing",
    )(docs, k, v)
    by_head = lax.all_to_all(trailing, ctx, 0, 0, tiled=True)

    low_bottom = lax.ppermute(bottom, "y", ring(1))
    high_top = lax.ppermute(top, "y", ring(-1))

    g, leading = pl.pallas_call(
        leading_kernel,
        grid=(HEADS // per,),
        in_specs=[
            SMEM,
            whole((TOKENS, width)),
            pl.BlockSpec((per * HDIM, width), lambda i: (i, 0)),
            block,
        ],
        out_specs=[block, summed],
        out_shape=[tokens, payload],
        compiler_params=params(),
        cost_estimate=cost(2 * 256 * 2048 * 2048, 12 << 20),
        name="leading",
    )(docs, go, weight, q)

    def scan(reverse, *parts):
        return pl.pallas_call(
            functools.partial(scan_kernel, reverse),
            out_shape=jax.ShapeDtypeStruct((BLOCKS, HDIM + ROWS * (len(parts) - 1), HDIM), F32),
            compiler_params=params(SMALL),
            cost_estimate=cost(1 << 20, 2 << 20),
            name="scan",
        )(*parts)

    by_head, leading, low_top, high_bottom = lax.optimization_barrier((by_head, leading, low_top, high_bottom))
    far_top = lax.ppermute(low_top, "y", ring(1))
    far_bottom = lax.ppermute(high_bottom, "y", ring(-1))
    state = lax.all_to_all(scan(False, by_head), ctx, 0, 0, tiled=True)
    leading, state, low_bottom, high_top = lax.optimization_barrier((leading, state, low_bottom, high_top))
    rev_by_head = lax.all_to_all(leading, ctx, 0, 0, tiled=True)

    def group(i, w):
        return (w[0] + 6 - i) % 4

    place = lax.axis_index("y").astype(jnp.int32).reshape(1)
    four = pl.BlockSpec((TOKENS, 4 * HDIM), lambda i, w: (0, group(i, w)))
    turned = jax.ShapeDtypeStruct((4 * HDIM, TOKENS), F32)
    attended, far, up, att_own, down = pl.pallas_call(
        attended_kernel,
        grid_spec=pltpu.PrefetchScalarGridSpec(
            num_scalar_prefetch=1,
            grid=(HEADS // 4,),
            in_specs=[SMEM, four, four, four, pl.BlockSpec((4, HDIM, HDIM), lambda i, w: (group(i, w), 0, 0))],
            out_specs=[four] + [pl.BlockSpec(part.shape, lambda i, w: (0, 0)) for part in (turned,) * 4],
            scratch_shapes=[pltpu.VMEM((4 * HDIM, TOKENS), F32)],
        ),
        out_shape=[tokens, turned, turned, jax.ShapeDtypeStruct(turned.shape, BF16), turned],
        compiler_params=params(SMALL),
        cost_estimate=cost(2 * 32 * 4 * 128**3, 7 << 20),
        name="attended",
    )(place, docs, q, k, v, state)
    rev_scan = scan(True, rev_by_head)
    far, up, down, far_top, far_bottom = lax.optimization_barrier((far, up, down, far_top, far_bottom))
    far = lax.ppermute(far, "y", ring(2))
    up = lax.ppermute(up, "y", ring(1))
    down = lax.ppermute(down, "y", ring(-1))
    far_top, rev_scan = lax.optimization_barrier((far_top, rev_scan))
    gathered = pack(
        go, (low_top, low_bottom, high_top, high_bottom, far_top, far_bottom)
    )

    layer_out = jnp.dot(attended, weight, preferred_element_type=F32).astype(BF16)

    core = lax.axis_index("core")
    rev = lax.all_to_all(rev_scan, ctx, 0, 0, tiled=True)
    atts = (att_own, up, down, far)
    given = product(atts, gathered, 1 - core)
    core, rev = lax.optimization_barrier((core, rev))
    kept = product(atts, gathered, core)
    taken = lax.ppermute(given, "core", [(0, 1), (1, 0)])
    spread = lax.all_to_all((kept + taken) * factor, ctx, 0, 0, tiled=True)
    grad_weight = jnp.sum(spread, axis=0)

    grad_q, grad_k, grad_v = pl.pallas_call(
        grads_kernel,
        grid=(HEADS // per,),
        in_specs=[SMEM, block, block, block, block, matrix, matrix],
        out_specs=[block, block, block],
        out_shape=[tokens, tokens, tokens],
        compiler_params=params(SMALL),
        cost_estimate=cost(2 * 32 * 10 * 128**3, 9 << 20),
        name="grads",
    )(docs, q, k, v, g, state, rev)
    return layer_out[None], grad_q[None], grad_k[None], grad_v[None], grad_weight


def solution(mesh):
    fine = Mesh(mesh.devices.reshape(4, 2, 4, 4), ("y", "core", "x", "z"))
    dp, ctx = ("y", "core"), ("x", "z")
    tokens = P(dp, ctx, None)
    return jax.shard_map(
        body,
        mesh=fine,
        in_specs=(tokens, tokens, tokens, P(), tokens, P(dp, ctx)),
        out_specs=(tokens, tokens, tokens, tokens, P(dp, ctx)),
        check_vma=False,
    )
```
